512 devices in a mesh: ctx: 64 (over y, z_lo, core), tp: 8 (over z_hi, x).
Axes of the slice: x: 4, y: 4, z: 16 (z_hi: 2, z_lo: 8; z = z_hi * 8 + z_lo), core: 2. Of those that a mesh axis runs over, the one named last changes fastest.
Arguments:
- qkv_values: bfloat16 [16384, 3, 8192], P('ctx', None, 'tp'), may hold values from -6 to 6
- short_taps: float32 [7, 3, 8192], P(None, None, 'tp'), may hold values from -2 to 2
- medium_taps: float32 [128, 8192], P(None, 'tp'), may hold values from -0.5 to 0.5
- skip_gain: float32 [8192], P('tp'), may hold values from -4 to 4
- out_weight: bfloat16 [8192, 4096], P('tp', 'ctx'), may hold values from -0.0625 to 0.0625
Outputs:
- block_out: bfloat16 [16384, 4096], P('ctx', 'tp')
The draws below stay inside these ranges and needn't reach their ends.
All inputs are finite; a program needn't handle non-finite values.
Results may differ from the reference program's by a relative error of at most 0.015.
Values may be sent and summed in bfloat16 or wider, within the bound.
A program may use at most 64 MiB of HBM per device.

```python
import jax
import jax.numpy as jnp
from jax import lax

C = 8192
D = 4096
TOK_DEV = 256
STAP = 7
MTAP = 128
TOKENS = 16384
N_CTX = 64
N_TP = 8


def block_scale(rng, shape, shards, smallest, top_value):
    level = 1.0
    for axis_at, parts in shards:
        draws = jax.random.uniform(jax.random.fold_in(jax.random.fold_in(rng, 6), axis_at), (parts,), jnp.float32, smallest / len(shards), top_value / len(shards))
        level = level * jnp.repeat(jnp.exp(draws), shape[axis_at] // parts).reshape((-1,) + (1,) * (len(shape) - 1 - axis_at))
    return level


def normal_values(stream_key, shape, width, reach, pieces=(), held_as=jnp.bfloat16):
    array = width * jax.random.normal(stream_key, shape, jnp.float32)
    if pieces:
        array = array * block_scale(stream_key, shape, pieces, -0.22, 0.18)
    return jnp.clip(array, -reach, reach).astype(held_as)


def setup_inputs(seed: int = 0) -> dict:
    splits = jax.random.split(jax.random.key(seed), 6)
    qkv_values = normal_values(splits[0], (TOKENS, 3, C), 1.0, 6.0, ((0, 64), (2, 8)))
    short_taps = normal_values(splits[1], (STAP, 3, C), STAP ** -0.5, 2.0, ((2, 8),), jnp.float32)
    medium_taps = normal_values(splits[2], (MTAP, C), MTAP ** -0.5, 0.5, ((1, 8),), jnp.float32)
    skip_gain = normal_values(splits[3], (C,), 1.0, 4.0, ((0, 8),), jnp.float32)
    out_weight = normal_values(splits[4], (C, D), C ** -0.5, 0.0625, ((0, 8), (1, 64)))
    return dict(qkv_values=qkv_values, short_taps=short_taps, medium_taps=medium_taps, skip_gain=skip_gain, out_weight=out_weight)


def causal_taps(signal, tap_table):
    tap_count = tap_table.shape[0]
    length = signal.shape[0]
    leading = jnp.zeros((tap_count - 1,) + signal.shape[1:], jnp.float32)
    padded = jnp.concatenate([leading, signal], axis=0)
    summed = jnp.zeros(signal.shape, jnp.float32)
    for offset in range(tap_count):
        window = lax.slice_in_dim(padded, tap_count - 1 - offset, tap_count - 1 - offset + length, axis=0)
        summed = summed + tap_table[offset] * window
    return summed


def reference(qkv_values, short_taps, medium_taps, skip_gain, out_weight):
    shortened = causal_taps(qkv_values.astype(jnp.float32), short_taps)
    queries = shortened[:, 0]
    product = shortened[:, 1] * shortened[:, 2]
    carried = causal_taps(product, medium_taps)
    gated_out = (queries * (carried + skip_gain * product)).astype(jnp.bfloat16)
    group_width = C // N_TP

    def project(row_block):
        summed = jnp.zeros((row_block.shape[0], D), jnp.float32)
        for block_index in range(N_TP):
            lower = block_index * group_width
            partial_value = jnp.dot(row_block[:, lower:lower + group_width], out_weight[lower:lower + group_width], preferred_element_type=jnp.float32)
            partial_value = lax.optimization_barrier(partial_value.astype(jnp.bfloat16)).astype(jnp.float32)
            summed = summed + partial_value
        return summed.astype(jnp.bfloat16)

    blocks = lax.map(project, gated_out.reshape(N_CTX, TOK_DEV, C))
    return blocks.reshape(TOKENS, D)
```

```python
import numpy as np
import jax
import jax.numpy as jnp
from jax import lax
from jax.experimental import pallas as pl
from jax.experimental.pallas import tpu as pltpu
from jax.sharding import PartitionSpec as P

MESH = pl.DeviceIdType.MESH
F32, BF16 = jnp.float32, jnp.bfloat16
NT = (((1,), (1,)), ((), ()))


def dft_tables():
    n = np.arange(256)
    k = np.arange(128)[:, None]
    angle = 2 * np.pi * ((k * n) % 256) / 256
    imag = -np.sin(angle)
    imag[0] = 1 - 2 * (n % 2)
    forward = np.concatenate([np.cos(angle), imag], axis=0)
    weight = np.full((256, 1), 2 / 256)
    weight[0] = weight[128] = 1 / 256
    inverse = (forward * weight).T[128:]

    def split(table):
        high = table.astype(jnp.bfloat16)
        return np.stack([high, (table - high.astype(np.float64)).astype(jnp.bfloat16)])

    return split(forward), split(inverse)


def dot(a, b):
    return jnp.dot(a, b, preferred_element_type=F32)


def kernel(q_hbm, st_hbm, mt_hbm, gain_hbm, w_hbm, f_hbm, i_hbm, out_ref,
           qv, st, mt, gain, fwd, inv, halo, streams, prod, px, query, spec, gated,
           wbuf, pb, xr, fin, zs_buf, zr_buf,
           load_sem, halo_send, halo_recv, wr, s_z, s_y, s_f, s_p, x_send, x_recv, zx_send, zx_recv):
    ctx, tp = lax.axis_index("ctx"), lax.axis_index("tp")
    y, z, c = ctx // 16, (ctx // 2) % 8, ctx % 2
    zh, x = tp // 4, tp % 4

    def dev(yy, zz, cc):
        return {"ctx": (yy * 8 + zz) * 2 + cc, "tp": tp}

    y_next, y_prev, y_far = (y + 1) % 4, (y + 3) % 4, (y + 2) % 4
    other_half = {"ctx": ctx, "tp": (1 - zh) * 4 + x}

    def block_index(ys, zs, cc):
        return (ys * 8 + zs) * 2 + cc

    def rows_of(b):
        return pl.ds(pl.multiple_of(b * 64, 64), 64)

    own = block_index(y, z, c)
    loads = [
        pltpu.make_async_copy(w_hbm, wbuf.at[rows_of(own)], load_sem.at[0]),
        pltpu.make_async_copy(q_hbm, qv, load_sem.at[1]),
        pltpu.make_async_copy(st_hbm, st, load_sem.at[2]),
        pltpu.make_async_copy(mt_hbm, mt, load_sem.at[3]),
        pltpu.make_async_copy(gain_hbm, gain, load_sem.at[4]),
        pltpu.make_async_copy(f_hbm, fwd, load_sem.at[5]),
        pltpu.make_async_copy(i_hbm, inv, load_sem.at[6]),
    ]
    for load in loads:
        load.start()

    barrier = pltpu.get_barrier_semaphore()

    def greet(target):
        pl.semaphore_signal(barrier, inc=1, device_id=target, device_id_type=MESH)

    greet(other_half)
    pl.when(ctx > 0)(lambda: greet({"ctx": ctx - 1, "tp": tp}))
    pl.when(z > 0)(lambda: greet(dev(y, z - 1, c)))
    pl.when(z < 7)(lambda: greet(dev(y, z + 1, c)))
    greet(dev(y_next, z, c))
    greet(dev(y_prev, z, c))
    for step in range(1, 4):
        greet({"ctx": ctx, "tp": zh * 4 + (x + step) % 4})
    greet(dev(y, z, 1 - c))
    loads[0].wait()
    loads[1].wait()
    pl.semaphore_wait(barrier, 7 + (1 - z // 7) + (z + 7) // 8 + (1 - ctx // 63))

    def remote(src, dst, send, recv, target):
        return pltpu.make_async_remote_copy(
            src_ref=src, dst_ref=dst, send_sem=send, recv_sem=recv, device_id=target, device_id_type=MESH)

    def block_copy(b, send, target, half=0, piece=None):
        rows = rows_of(b) if piece is None else pl.ds(pl.multiple_of(b * 64 + piece * 32, 32), 32)
        return remote(wbuf.at[rows], wbuf.at[rows], send, wr.at[b, half], target)

    def z_up(zs):
        return block_copy(block_index(y, zs, c), s_z.at[0, zs], dev(y, z + 1, c))

    def z_down(zs):
        return block_copy(block_index(y, zs, c), s_z.at[1, zs], dev(y, z - 1, c))

    def y_up(zs):
        return block_copy(block_index(y, zs, c), s_y.at[0, zs], dev(y_next, z, c))

    def y_down(zs):
        return block_copy(block_index(y, zs, c), s_y.at[1, zs], dev(y_prev, z, c))

    def y_on_up(zs):
        return block_copy(block_index(y_prev, zs, c), s_f.at[0, zs], dev(y_next, z, c), 0, 0)

    def y_on_down(zs):
        return block_copy(block_index(y_next, zs, c), s_f.at[1, zs], dev(y_prev, z, c), 1, 1)

    def to_partner(ys, zs):
        return block_copy(block_index(ys, zs, c), s_p.at[ys, zs], dev(y, z, 1 - c))

    def arrived(b, half=0, piece=None):
        block_copy(b, s_p.at[0, 0], dev(y, z, 1 - c), half, piece).wait_recv()

    low = 1 - z // 4
    near = z * low + (7 - z) * (1 - low)

    def place(k):
        far = (k - 2 * near + 15) // 16
        return z + (1 - far) * ((k + 1) // 2) * (1 - 2 * ((k + 1) % 2)) + far * (k - near) * (2 * low - 1)

    def step_z(k, first=False):
        zs = z if first else place(k)
        if not first:
            arrived(block_index(y, zs, c))
        pl.when((zs <= z) & (z < 7))(lambda: z_up(zs).start())
        pl.when((zs >= z) & (z > 0))(lambda: z_down(zs).start())
        y_up(zs).start()
        y_down(zs).start()
        to_partner(y, zs).start()

    def step_y(k):
        zs = place(k)
        arrived(block_index(y_prev, zs, c))
        y_on_up(zs).start()
        to_partner(y_prev, zs).start()
        arrived(block_index(y_next, zs, c))
        y_on_down(zs).start()
        to_partner(y_next, zs).start()

    def step_y_far(k):
        zs = place(k)
        arrived(block_index(y_far, zs, c), 0, 0)
        arrived(block_index(y_far, zs, c), 1, 1)
        to_partner(y_far, zs).start()

    def x_copy(owner, slot):
        return remote(pb.at[owner, slot], xr.at[(x - owner + 4) % 4 - 1, slot], x_send.at[owner, slot],
                      x_recv.at[(x - owner + 4) % 4 - 1, slot], {"ctx": ctx, "tp": zh * 4 + owner})

    def z_copy(i):
        return remote(zs_buf.at[i], zr_buf.at[i], zx_send.at[i], zx_recv.at[i], other_half)

    def unit(k, dy):
        zs, ys = place(k), (y + dy) % 4
        arrived(block_index(ys, zs, 1 - c))
        block = wbuf[pl.ds(pl.multiple_of((ys * 8 + zs) * 128, 128), 128), :]
        part = lax.dot_general(gated[...], block, NT, preferred_element_type=F32)
        owner, slot = (ys % 2) * 2 + zs // 4, (ys // 2) * 4 + zs % 4
        pb[owner, slot] = part.astype(BF16)
        pl.when(owner != x)(lambda: x_copy(owner, slot).start())

    def gather_sum(k, dy):
        zs, ys = place(k), (y + dy) % 4
        owner, slot, i = (ys % 2) * 2 + zs // 4, (ys // 2) * 4 + zs % 4, zs % 4

        @pl.when(owner == x)
        def _():
            for s in range(3):
                remote(pb.at[0, 0], xr.at[s, slot], x_send.at[0, 0], x_recv.at[s, slot], other_half).wait_recv()
            total = pb[x, slot].astype(F32)
            for s in range(3):
                total = total + xr[s, slot].astype(F32)

            @pl.when(ys // 2 == zh)
            def _():
                fin[i] = total

            @pl.when(ys // 2 != zh)
            def _():
                zs_buf[i] = total.astype(BF16)
                z_copy(i).start()

    step_z(0, first=True)

    following = {"ctx": ctx + 1, "tp": tp}
    tail_copy = remote(qv.at[:, pl.ds(240, 16), :], halo, halo_send.at[0], halo_recv.at[0], following)
    prod_copy = remote(px.at[pl.ds(256, 128)], px.at[pl.ds(0, 128)], halo_send.at[1], halo_recv.at[1], following)
    pl.when(ctx < 63)(lambda: tail_copy.start())
    loads[2].wait()

    def lanes(ch, width=128):
        return pl.ds(pl.multiple_of(ch * width, width), width)

    def short(i, ch, first, count):
        total = None
        for j in range(7):
            term = st[i, j:j + 1, lanes(ch)] * streams[i, ch, pl.ds(16 + first - j, count), :]
            total = term if total is None else total + term
        return total

    def conv_late(ch, carry):
        for i in (1, 2):
            streams[i, ch, 16:272, :] = qv[i, :, lanes(ch)].astype(F32)
        value = short(1, ch, 128, 128) * short(2, ch, 128, 128)
        prod[128:256, lanes(ch)] = value
        px[256:384, lanes(ch)] = value.astype(BF16)
        return carry

    lax.fori_loop(0, 8, conv_late, 0)
    pl.when(ctx < 63)(lambda: prod_copy.start())

    step_z(1)

    @pl.when(ctx > 0)
    def _():
        tail_copy.wait_recv()

    @pl.when(ctx == 0)
    def _():
        halo[...] = jnp.zeros_like(halo)
        px[0:128, :] = jnp.zeros((128, 1024), BF16)

    def conv_early(ch, carry):
        for i in range(3):
            streams[i, ch, 0:16, :] = halo[i, :, lanes(ch)].astype(F32)
        streams[0, ch, 16:272, :] = qv[0, :, lanes(ch)].astype(F32)
        value = short(1, ch, 0, 128) * short(2, ch, 0, 128)
        prod[0:128, lanes(ch)] = value
        px[128:256, lanes(ch)] = value.astype(BF16)
        query[0:128, lanes(ch)] = short(0, ch, 0, 128)
        query[128:256, lanes(ch)] = short(0, ch, 128, 128)
        return carry

    lax.fori_loop(0, 8, conv_early, 0)
    step_z(2)
    step_y(0)

    for load in loads[3:]:
        load.wait()
    pl.when(ctx > 0)(lambda: prod_copy.wait_recv())

    def medium(group, carry):
        at = lanes(group, 256)
        taps = mt[:, at]
        taps_high = taps.astype(BF16)
        taps_low = (taps - taps_high.astype(F32)).astype(BF16)
        spectrum = (dot(fwd[0, :, 0:128], taps_high) + dot(fwd[0, :, 0:128], taps_low)
                    + dot(fwd[1, :, 0:128], taps_high))
        first = lax.broadcasted_iota(jnp.int32, (128, 256), 0) == 0
        h_real, h_imag = spectrum[0:128], spectrum[128:256]
        h_cross = jnp.where(first, 0.0, h_imag)
        h_last = jnp.where(first, h_imag, h_real)
        for part in range(2):
            seg = px[128 * part:128 * part + 256, at]
            x_all = dot(fwd[0], seg) + dot(fwd[1], seg)
            x_real, x_imag = x_all[0:128], x_all[128:256]
            spec[0:128, :] = x_real * h_real - x_imag * h_cross
            spec[128:256, :] = x_real * h_cross + x_imag * h_last
            whole = spec[...]
            high = whole.astype(BF16)
            low_part = (whole - high.astype(F32)).astype(BF16)
            carried = dot(inv[0], high) + dot(inv[0], low_part) + dot(inv[1], high)
            here = slice(128 * part, 128 * part + 128)
            gated[here, at] = (query[here, at] * (carried + gain[0:1, at] * prod[here, at])).astype(BF16)
        return carry

    lax.fori_loop(0, 4, medium, 0)

    def main(t, carry):
        pl.when(t < 8)(lambda: step_z(t))
        pl.when(t < 10)(lambda: step_y(t - 2))
        pl.when(t < 11)(lambda: step_y_far(t - 3))

        @pl.when(t < 11)
        def _():
            for dy in (0, 1, 3):
                unit(t - 3, dy)

        @pl.when((t >= 4) & (t < 12))
        def _():
            unit(t - 4, 2)
            for dy in (0, 1, 3):
                gather_sum(t - 4, dy)

        @pl.when(t >= 5)
        def _():
            gather_sum(t - 5, 2)

        return carry

    lax.fori_loop(3, 13, main, 0)

    for i in range(4):
        z_copy(i).wait_recv()
        out_ref[:, 128 * i:128 * i + 128] = (fin[i] + zr_buf[i].astype(F32)).astype(BF16)

    def drain(zs, carry):
        pl.when((zs <= z) & (z < 7))(lambda: z_up(zs).wait_send())
        pl.when((zs >= z) & (z > 0))(lambda: z_down(zs).wait_send())
        for copy in (y_up, y_down, y_on_up, y_on_down):
            copy(zs).wait_send()
        for ys in range(4):
            to_partner(ys, zs).wait_send()
        for step in range(1, 4):
            x_copy((x + step) % 4, zs).wait_send()
        return carry

    lax.fori_loop(0, 8, drain, 0)
    for i in range(4):
        z_copy(i).wait_send()

    @pl.when(ctx < 63)
    def _():
        tail_copy.wait_send()
        prod_copy.wait_send()


def on_device(qkv_values, short_taps, medium_taps, skip_gain, out_weight):
    forward, inverse = dft_tables()
    dma = pltpu.SemaphoreType.DMA
    return pl.pallas_call(
        kernel,
        out_shape=jax.ShapeDtypeStruct((256, 512), BF16),
        in_specs=[pl.BlockSpec(memory_space=pl.ANY)] * 7,
        out_specs=pl.BlockSpec(memory_space=pltpu.VMEM),
        scratch_shapes=[
            pltpu.VMEM((3, 256, 1024), BF16),
            pltpu.VMEM((3, 7, 1024), F32),
            pltpu.VMEM((128, 1024), F32),
            pltpu.VMEM((1, 1024), F32),
            pltpu.VMEM((2, 256, 256), BF16),
            pltpu.VMEM((2, 128, 256), BF16),
            pltpu.VMEM((3, 16, 1024), BF16),
            pltpu.VMEM((3, 8, 272, 128), F32),
            pltpu.VMEM((256, 1024), F32),
            pltpu.VMEM((384, 1024), BF16),
            pltpu.VMEM((256, 1024), F32),
            pltpu.VMEM((256, 256), F32),
            pltpu.VMEM((256, 1024), BF16),
            pltpu.VMEM((4096, 1024), BF16),
            pltpu.VMEM((4, 8, 256, 128), BF16),
            pltpu.VMEM((3, 8, 256, 128), BF16),
            pltpu.VMEM((4, 256, 128), F32),
            pltpu.VMEM((4, 256, 128), BF16),
            pltpu.VMEM((4, 256, 128), BF16),
            dma((7,)),
            dma((2,)), dma((2,)),
            dma((64, 2)),
            dma((2, 8)), dma((2, 8)), dma((2, 8)), dma((4, 8)),
            dma((4, 8)), dma((3, 8)),
            dma((4,)), dma((4,)),
        ],
        compiler_params=pltpu.CompilerParams(
            collective_id=0, has_side_effects=True, vmem_limit_bytes=48 * 2**20),
        cost_estimate=pl.CostEstimate(flops=3 * 10**9, bytes_accessed=4 * 10**6, transcendentals=0),
    )(
        jnp.transpose(qkv_values, (1, 0, 2)),
        jnp.transpose(short_taps, (1, 0, 2)),
        medium_taps,
        skip_gain.reshape(1, -1),
        out_weight.T,
        jnp.asarray(forward),
        jnp.asarray(inverse),
    )


def solution(mesh):
    return jax.shard_map(
        on_device,
        mesh=mesh,
        in_specs=(
            P("ctx", None, "tp"),
            P(None, None, "tp"),
            P(None, "tp"),
            P("tp"),
            P("tp", "ctx"),
        ),
        out_specs=P("ctx", "tp"),
        check_vma=False,
    )
```

```python
import numpy as np
import jax
import jax.numpy as jnp
from jax import lax
from jax.experimental import pallas as pl
from jax.experimental.pallas import tpu as pltpu
from jax.sharding import PartitionSpec as P

MESH = pl.DeviceIdType.MESH
F32, BF16 = jnp.float32, jnp.bfloat16
NT = (((1,), (1,)), ((), ()))


def dft_tables():
    n = np.arange(256)
    k = np.arange(128)[:, None]
    angle = 2 * np.pi * ((k * n) % 256) / 256
    imag = -np.sin(angle)
    imag[0] = 1 - 2 * (n % 2)
    forward = np.concatenate([np.cos(angle), imag], axis=0)
    weight = np.full((256, 1), 2 / 256)
    weight[0] = weight[128] = 1 / 256
    inverse = (forward * weight).T[128:]

    def split(table):
        high = table.astype(jnp.bfloat16)
        return np.stack([high, (table - high.astype(np.float64)).astype(jnp.bfloat16)])

    return split(forward), split(inverse)


def dot(a, b):
    return jnp.dot(a, b, preferred_element_type=F32)


def kernel(q_hbm, st_hbm, mt_hbm, gain_hbm, w_hbm, f_hbm, i_hbm, out_ref,
           qv, st, mt, gain, fwd, inv, halo, streams, prod, px, query, spec, gated,
           wbuf, pb, xf, xr, fin, zs_buf, zr_buf,
           load_sem, halo_send, halo_recv, wr, s_z, s_y, s_f, s_p, xf_send, xf_recv, xd_send, xd_recv, xl_send, xl_recv, zx_send, zx_recv):
    ctx, tp = lax.axis_index("ctx"), lax.axis_index("tp")
    y, z, c = ctx // 16, (ctx // 2) % 8, ctx % 2
    zh, x = tp // 4, tp % 4

    def dev(yy, zz, cc):
        return {"ctx": (yy * 8 + zz) * 2 + cc, "tp": tp}

    y_next, y_prev, y_far = (y + 1) % 4, (y + 3) % 4, (y + 2) % 4
    other_half = {"ctx": ctx, "tp": (1 - zh) * 4 + x}

    def block_index(ys, zs, cc):
        return (ys * 8 + zs) * 2 + cc

    def rows_of(b):
        return pl.ds(pl.multiple_of(b * 64, 64), 64)

    own = block_index(y, z, c)
    loads = [
        pltpu.make_async_copy(w_hbm, wbuf.at[rows_of(own)], load_sem.at[0]),
        pltpu.make_async_copy(q_hbm, qv, load_sem.at[1]),
        pltpu.make_async_copy(st_hbm, st, load_sem.at[2]),
        pltpu.make_async_copy(mt_hbm, mt, load_sem.at[3]),
        pltpu.make_async_copy(gain_hbm, gain, load_sem.at[4]),
        pltpu.make_async_copy(f_hbm, fwd, load_sem.at[5]),
        pltpu.make_async_copy(i_hbm, inv, load_sem.at[6]),
    ]
    for load in loads:
        load.start()

    barrier = pltpu.get_barrier_semaphore()

    def greet(target):
        pl.semaphore_signal(barrier, inc=1, device_id=target, device_id_type=MESH)

    greet(other_half)
    pl.when(ctx > 0)(lambda: greet({"ctx": ctx - 1, "tp": tp}))
    pl.when(z > 0)(lambda: greet(dev(y, z - 1, c)))
    pl.when(z < 7)(lambda: greet(dev(y, z + 1, c)))
    greet(dev(y_next, z, c))
    greet(dev(y_prev, z, c))
    for step in range(1, 4):
        greet({"ctx": ctx, "tp": zh * 4 + (x + step) % 4})
    greet(dev(y, z, 1 - c))
    loads[0].wait()
    loads[1].wait()
    pl.semaphore_wait(barrier, 7 + (1 - z // 7) + (z + 7) // 8 + (1 - ctx // 63))

    def remote(src, dst, send, recv, target):
        return pltpu.make_async_remote_copy(
            src_ref=src, dst_ref=dst, send_sem=send, recv_sem=recv, device_id=target, device_id_type=MESH)

    def block_copy(b, send, target, half=0, piece=None):
        rows = rows_of(b) if piece is None else pl.ds(pl.multiple_of(b * 64 + piece * 32, 32), 32)
        return remote(wbuf.at[rows], wbuf.at[rows], send, wr.at[b, half], target)

    def z_up(zs, piece):
        return block_copy(block_index(y, zs, c), s_z.at[0, zs, piece], dev(y, z + 1, c), piece, piece)

    def z_down(zs, piece):
        return block_copy(block_index(y, zs, c), s_z.at[1, zs, piece], dev(y, z - 1, c), piece, piece)

    def y_up(zs):
        return block_copy(block_index(y, zs, c), s_y.at[0, zs], dev(y_next, z, c))

    def y_down(zs):
        return block_copy(block_index(y, zs, c), s_y.at[1, zs], dev(y_prev, z, c))

    def y_on_up(zs):
        return block_copy(block_index(y_prev, zs, c), s_f.at[0, zs], dev(y_next, z, c), 0, 0)

    def y_on_down(zs):
        return block_copy(block_index(y_next, zs, c), s_f.at[1, zs], dev(y_prev, z, c), 1, 1)

    def to_partner(ys, zs):
        return block_copy(block_index(ys, zs, c), s_p.at[ys, zs], dev(y, z, 1 - c))

    def arrived(b, half=0, piece=None):
        block_copy(b, s_p.at[0, 0], dev(y, z, 1 - c), half, piece).wait_recv()

    low = 1 - z // 4
    near = z * low + (7 - z) * (1 - low)

    def place(k):
        far = (k - 2 * near + 15) // 16
        return z + (1 - far) * ((k + 1) // 2) * (1 - 2 * ((k + 1) % 2)) + far * (k - near) * (2 * low - 1)

    def spread(zs):
        y_up(zs).start()
        y_down(zs).start()
        to_partner(y, zs).start()

    def step_z(distance):
        @pl.when(z >= distance)
        def _():
            zs = z - distance
            for piece in range(2):
                arrived(block_index(y, zs, c), piece, piece)
                pl.when(z < 7)(lambda: z_up(zs, piece).start())
            spread(zs)

        @pl.when(z + distance < 8)
        def _():
            zs = z + distance
            for piece in range(2):
                arrived(block_index(y, zs, c), piece, piece)
                pl.when(z > 0)(lambda: z_down(zs, piece).start())
            spread(zs)

    def step_y(k):
        zs = place(k)
        arrived(block_index(y_prev, zs, c))
        y_on_up(zs).start()
        to_partner(y_prev, zs).start()
        arrived(block_index(y_next, zs, c))
        y_on_down(zs).start()
        to_partner(y_next, zs).start()

    def step_y_far(k):
        zs = place(k)
        arrived(block_index(y_far, zs, c), 0, 0)
        arrived(block_index(y_far, zs, c), 1, 1)
        to_partner(y_far, zs).start()

    def side(slot):
        return 2 * ((slot // 4 + slot) % 2)

    def along_x(place):
        return {"ctx": ctx, "tp": zh * 4 + place % 4}

    def far_copy(slot):
        return remote(pb.at[(x + 2) % 4, slot], xf.at[slot], xf_send.at[slot], xf_recv.at[slot],
                      along_x(x + 3 + side(slot)))

    def direct_copy(slot):
        owner = (x + 1 + side(slot)) % 4
        return remote(pb.at[owner, slot], xr.at[0, slot], xd_send.at[slot], xd_recv.at[slot], along_x(owner))

    def relay_copy(slot):
        owner = (x + 3 + side(slot)) % 4
        return remote(pb.at[owner, slot], xr.at[1, slot], xl_send.at[slot], xl_recv.at[slot], along_x(owner))

    def z_copy(i):
        return remote(zs_buf.at[i], zr_buf.at[i], zx_send.at[i], zx_recv.at[i], other_half)

    def unit(k, dy):
        zs, ys = place(k), (y + dy) % 4
        arrived(block_index(ys, zs, 1 - c))
        block = wbuf[pl.ds(pl.multiple_of((ys * 8 + zs) * 128, 128), 128), :]
        part = lax.dot_general(gated[...], block, NT, preferred_element_type=F32)
        owner, slot = (ys % 2) * 2 + zs // 4, (ys // 2) * 4 + zs % 4
        pb[owner, slot] = part.astype(BF16)
        pl.when(owner == (x + 2) % 4)(lambda: far_copy(slot).start())
        pl.when(owner == (x + 1 + side(slot)) % 4)(lambda: direct_copy(slot).start())

    def relay(k, dy):
        zs, ys = place(k), (y + dy) % 4
        owner, slot = (ys % 2) * 2 + zs // 4, (ys // 2) * 4 + zs % 4

        @pl.when(owner == (x + 3 + side(slot)) % 4)
        def _():
            far_copy(slot).wait_recv()
            pb[owner, slot] = (pb[owner, slot].astype(F32) + xf[slot].astype(F32)).astype(BF16)
            relay_copy(slot).start()

    def gather_sum(k, dy):
        zs, ys = place(k), (y + dy) % 4
        owner, slot, i = (ys % 2) * 2 + zs // 4, (ys // 2) * 4 + zs % 4, zs % 4

        @pl.when(owner == x)
        def _():
            direct_copy(slot).wait_recv()
            relay_copy(slot).wait_recv()
            total = pb[x, slot].astype(F32) + xr[0, slot].astype(F32) + xr[1, slot].astype(F32)

            @pl.when(ys // 2 == zh)
            def _():
                fin[i] = total

            @pl.when(ys // 2 != zh)
            def _():
                zs_buf[i] = total.astype(BF16)
                z_copy(i).start()

    for piece in range(2):
        pl.when(z < 7)(lambda: z_up(z, piece).start())
        pl.when(z > 0)(lambda: z_down(z, piece).start())
    spread(z)

    following = {"ctx": ctx + 1, "tp": tp}
    tail_copy = remote(qv.at[:, pl.ds(240, 16), :], halo, halo_send.at[0], halo_recv.at[0], following)
    prod_copy = remote(px.at[pl.ds(256, 128)], px.at[pl.ds(0, 128)], halo_send.at[1], halo_recv.at[1], following)
    pl.when(ctx < 63)(lambda: tail_copy.start())
    loads[2].wait()

    def lanes(ch, width=128):
        return pl.ds(pl.multiple_of(ch * width, width), width)

    def short(i, ch, first, count):
        total = None
        for j in range(7):
            term = st[i, j:j + 1, lanes(ch)] * streams[i, ch, pl.ds(16 + first - j, count), :]
            total = term if total is None else total + term
        return total

    def conv_late(ch, carry):
        for i in (1, 2):
            streams[i, ch, 16:272, :] = qv[i, :, lanes(ch)].astype(F32)
        value = short(1, ch, 128, 128) * short(2, ch, 128, 128)
        prod[128:256, lanes(ch)] = value
        px[256:384, lanes(ch)] = value.astype(BF16)
        return carry

    lax.fori_loop(0, 8, conv_late, 0)
    pl.when(ctx < 63)(lambda: prod_copy.start())

    step_z(1)

    @pl.when(ctx > 0)
    def _():
        tail_copy.wait_recv()

    @pl.when(ctx == 0)
    def _():
        halo[...] = jnp.zeros_like(halo)
        px[0:128, :] = jnp.zeros((128, 1024), BF16)

    def conv_early(ch, carry):
        for i in range(3):
            streams[i, ch, 0:16, :] = halo[i, :, lanes(ch)].astype(F32)
        streams[0, ch, 16:272, :] = qv[0, :, lanes(ch)].astype(F32)
        value = short(1, ch, 0, 128) * short(2, ch, 0, 128)
        prod[0:128, lanes(ch)] = value
        px[128:256, lanes(ch)] = value.astype(BF16)
        query[0:128, lanes(ch)] = short(0, ch, 0, 128)
        query[128:256, lanes(ch)] = short(0, ch, 128, 128)
        return carry

    lax.fori_loop(0, 8, conv_early, 0)
    step_z(2)
    step_y(0)

    for load in loads[3:]:
        load.wait()
    pl.when(ctx > 0)(lambda: prod_copy.wait_recv())

    def medium(group, carry):
        at = lanes(group, 256)
        taps = mt[:, at]
        taps_high = taps.astype(BF16)
        taps_low = (taps - taps_high.astype(F32)).astype(BF16)
        spectrum = (dot(fwd[0, :, 0:128], taps_high) + dot(fwd[0, :, 0:128], taps_low)
                    + dot(fwd[1, :, 0:128], taps_high))
        first = lax.broadcasted_iota(jnp.int32, (128, 256), 0) == 0
        h_real, h_imag = spectrum[0:128], spectrum[128:256]
        h_cross = jnp.where(first, 0.0, h_imag)
        h_last = jnp.where(first, h_imag, h_real)
        for part in range(2):
            seg = px[128 * part:128 * part + 256, at]
            x_all = dot(fwd[0], seg) + dot(fwd[1], seg)
            x_real, x_imag = x_all[0:128], x_all[128:256]
            spec[0:128, :] = x_real * h_real - x_imag * h_cross
            spec[128:256, :] = x_real * h_cross + x_imag * h_last
            whole = spec[...]
            high = whole.astype(BF16)
            low_part = (whole - high.astype(F32)).astype(BF16)
            carried = dot(inv[0], high) + dot(inv[0], low_part) + dot(inv[1], high)
            here = slice(128 * part, 128 * part + 128)
            gated[here, at] = (query[here, at] * (carried + gain[0:1, at] * prod[here, at])).astype(BF16)
        return carry

    lax.fori_loop(0, 4, medium, 0)

    def within(t, lag, run):
        pl.when((t >= lag) & (t < 8 + lag))(lambda: run(t - lag))

    def beside(run):
        def three(k):
            for dy in (0, 1, 3):
                run(k, dy)
        return three

    def across(run):
        return lambda k: run(k, 2)

    def main(t, carry):
        within(t, 0, step_z)
        within(t, 2, step_y)
        within(t, 4, step_y_far)
        within(t, 3, beside(unit))
        within(t, 5, beside(relay))
        within(t, 7, beside(gather_sum))
        within(t, 5, across(unit))
        within(t, 7, across(relay))
        within(t, 9, across(gather_sum))
        return carry

    lax.fori_loop(3, 17, main, 0)

    for i in range(4):
        z_copy(i).wait_recv()
        out_ref[:, 128 * i:128 * i + 128] = (fin[i] + zr_buf[i].astype(F32)).astype(BF16)

    def drain(zs, carry):
        for piece in range(2):
            pl.when((zs <= z) & (z < 7))(lambda: z_up(zs, piece).wait_send())
            pl.when((zs >= z) & (z > 0))(lambda: z_down(zs, piece).wait_send())
        for copy in (y_up, y_down, y_on_up, y_on_down):
            copy(zs).wait_send()
        for ys in range(4):
            to_partner(ys, zs).wait_send()
        for copy in (far_copy, direct_copy, relay_copy):
            copy(zs).wait_send()
        return carry

    lax.fori_loop(0, 8, drain, 0)
    for i in range(4):
        z_copy(i).wait_send()

    @pl.when(ctx < 63)
    def _():
        tail_copy.wait_send()
        prod_copy.wait_send()


def on_device(qkv_values, short_taps, medium_taps, skip_gain, out_weight):
    forward, inverse = dft_tables()
    dma = pltpu.SemaphoreType.DMA
    return pl.pallas_call(
        kernel,
        out_shape=jax.ShapeDtypeStruct((256, 512), BF16),
        in_specs=[pl.BlockSpec(memory_space=pl.ANY)] * 7,
        out_specs=pl.BlockSpec(memory_space=pltpu.VMEM),
        scratch_shapes=[
            pltpu.VMEM((3, 256, 1024), BF16),
            pltpu.VMEM((3, 7, 1024), F32),
            pltpu.VMEM((128, 1024), F32),
            pltpu.VMEM((1, 1024), F32),
            pltpu.VMEM((2, 256, 256), BF16),
            pltpu.VMEM((2, 128, 256), BF16),
            pltpu.VMEM((3, 16, 1024), BF16),
            pltpu.VMEM((3, 8, 272, 128), F32),
            pltpu.VMEM((256, 1024), F32),
            pltpu.VMEM((384, 1024), BF16),
            pltpu.VMEM((256, 1024), F32),
            pltpu.VMEM((256, 256), F32),
            pltpu.VMEM((256, 1024), BF16),
            pltpu.VMEM((4096, 1024), BF16),
            pltpu.VMEM((4, 8, 256, 128), BF16),
            pltpu.VMEM((8, 256, 128), BF16),
            pltpu.VMEM((2, 8, 256, 128), BF16),
            pltpu.VMEM((4, 256, 128), F32),
            pltpu.VMEM((4, 256, 128), BF16),
            pltpu.VMEM((4, 256, 128), BF16),
            dma((7,)),
            dma((2,)), dma((2,)),
            dma((64, 2)),
            dma((2, 8, 2)), dma((2, 8)), dma((2, 8)), dma((4, 8)),
            dma((8,)), dma((8,)), dma((8,)), dma((8,)), dma((8,)), dma((8,)),
            dma((4,)), dma((4,)),
        ],
        compiler_params=pltpu.CompilerParams(
            collective_id=0, has_side_effects=True, vmem_limit_bytes=63 * 2**20),
        cost_estimate=pl.CostEstimate(flops=3 * 10**9, bytes_accessed=4 * 10**6, transcendentals=0),
    )(
        jnp.transpose(qkv_values, (1, 0, 2)),
        jnp.transpose(short_taps, (1, 0, 2)),
        medium_taps,
        skip_gain.reshape(1, -1),
        out_weight.T,
        jnp.asarray(forward),
        jnp.asarray(inverse),
    )


def solution(mesh):
    return jax.shard_map(
        on_device,
        mesh=mesh,
        in_specs=(
            P("ctx", None, "tp"),
            P(None, None, "tp"),
            P(None, "tp"),
            P("tp"),
            P("tp", "ctx"),
        ),
        out_specs=P("ctx", "tp"),
        check_vma=False,
    )
```

```python
import numpy as np
import jax
import jax.numpy as jnp
from jax import lax
from jax.experimental import pallas as pl
from jax.experimental.pallas import tpu as pltpu
from jax.sharding import PartitionSpec as P

MESH = pl.DeviceIdType.MESH
F32, BF16 = jnp.float32, jnp.bfloat16
NT = (((1,), (1,)), ((), ()))


def dft_tables():
    n = np.arange(256)
    k = np.arange(128)[:, None]
    angle = 2 * np.pi * ((k * n) % 256) / 256
    imag = -np.sin(angle)
    imag[0] = 1 - 2 * (n % 2)
    forward = np.concatenate([np.cos(angle), imag], axis=0)
    weight = np.full((256, 1), 2 / 256)
    weight[0] = weight[128] = 1 / 256
    inverse = (forward * weight).T[128:]

    def split(table):
        high = table.astype(jnp.bfloat16)
        return np.stack([high, (table - high.astype(np.float64)).astype(jnp.bfloat16)])

    return split(forward), split(inverse)


def dot(a, b):
    return jnp.dot(a, b, preferred_element_type=F32)


def kernel(q_hbm, st_hbm, mt_hbm, gain_hbm, w_hbm, f_hbm, i_hbm, out_ref,
           qv, st, mt, gain, fwd, inv, halo, streams, prod, px, query, spec, gated,
           wbuf, pb, xf, xr, fin, zs_buf, zr_buf,
           load_sem, halo_send, halo_recv, wr, s_z, s_y, s_f, s_p, xf_send, xf_recv, xd_send, xd_recv, xl_send, xl_recv, zx_send, zx_recv):
    ctx, tp = lax.axis_index("ctx"), lax.axis_index("tp")
    y, z, c = ctx // 16, (ctx // 2) % 8, ctx % 2
    zh, x = tp // 4, tp % 4

    def dev(yy, zz, cc):
        return {"ctx": (yy * 8 + zz) * 2 + cc, "tp": tp}

    y_next, y_prev, y_far = (y + 1) % 4, (y + 3) % 4, (y + 2) % 4
    other_half = {"ctx": ctx, "tp": (1 - zh) * 4 + x}

    def block_index(ys, zs, cc):
        return (ys * 8 + zs) * 2 + cc

    def rows_of(b):
        return pl.ds(pl.multiple_of(b * 64, 64), 64)

    own = block_index(y, z, c)
    loads = [
        pltpu.make_async_copy(w_hbm, wbuf.at[rows_of(own)], load_sem.at[0]),
        pltpu.make_async_copy(q_hbm, qv, load_sem.at[1]),
        pltpu.make_async_copy(st_hbm, st, load_sem.at[2]),
        pltpu.make_async_copy(mt_hbm, mt, load_sem.at[3]),
        pltpu.make_async_copy(gain_hbm, gain, load_sem.at[4]),
        pltpu.make_async_copy(f_hbm, fwd, load_sem.at[5]),
        pltpu.make_async_copy(i_hbm, inv, load_sem.at[6]),
    ]
    for load in loads:
        load.start()

    barrier = pltpu.get_barrier_semaphore()

    def greet(target):
        pl.semaphore_signal(barrier, inc=1, device_id=target, device_id_type=MESH)

    greet(other_half)
    pl.when(ctx > 0)(lambda: greet({"ctx": ctx - 1, "tp": tp}))
    pl.when(z > 0)(lambda: greet(dev(y, z - 1, c)))
    pl.when(z < 7)(lambda: greet(dev(y, z + 1, c)))
    greet(dev(y_next, z, c))
    greet(dev(y_prev, z, c))
    for step in range(1, 4):
        greet({"ctx": ctx, "tp": zh * 4 + (x + step) % 4})
    greet(dev(y, z, 1 - c))
    loads[0].wait()
    loads[1].wait()
    pl.semaphore_wait(barrier, 7 + (1 - z // 7) + (z + 7) // 8 + (1 - ctx // 63))

    def remote(src, dst, send, recv, target):
        return pltpu.make_async_remote_copy(
            src_ref=src, dst_ref=dst, send_sem=send, recv_sem=recv, device_id=target, device_id_type=MESH)

    def block_copy(b, send, target, half=0, piece=None):
        rows = rows_of(b) if piece is None else pl.ds(pl.multiple_of(b * 64 + piece * 32, 32), 32)
        return remote(wbuf.at[rows], wbuf.at[rows], send, wr.at[b, half], target)

    def z_up(zs, piece):
        return block_copy(block_index(y, zs, c), s_z.at[0, zs, piece], dev(y, z + 1, c), piece, piece)

    def z_down(zs, piece):
        return block_copy(block_index(y, zs, c), s_z.at[1, zs, piece], dev(y, z - 1, c), piece, piece)

    def y_up(zs):
        return block_copy(block_index(y, zs, c), s_y.at[0, zs], dev(y_next, z, c))

    def y_down(zs):
        return block_copy(block_index(y, zs, c), s_y.at[1, zs], dev(y_prev, z, c))

    def y_on_up(zs):
        return block_copy(block_index(y_prev, zs, c), s_f.at[0, zs], dev(y_next, z, c), 0, 0)

    def y_on_down(zs):
        return block_copy(block_index(y_next, zs, c), s_f.at[1, zs], dev(y_prev, z, c), 1, 1)

    def to_partner(ys, zs):
        return block_copy(block_index(ys, zs, c), s_p.at[ys, zs], dev(y, z, 1 - c))

    def arrived(b, half=0, piece=None):
        block_copy(b, s_p.at[0, 0], dev(y, z, 1 - c), half, piece).wait_recv()

    low = 1 - z // 4
    near = z * low + (7 - z) * (1 - low)

    def place(k):
        far = (k - 2 * near + 15) // 16
        return z + (1 - far) * ((k + 1) // 2) * (1 - 2 * ((k + 1) % 2)) + far * (k - near) * (2 * low - 1)

    def spread(zs):
        y_up(zs).start()
        y_down(zs).start()
        to_partner(y, zs).start()

    def step_z(distance):
        @pl.when(z >= distance)
        def _():
            zs = z - distance
            for piece in range(2):
                arrived(block_index(y, zs, c), piece, piece)
                pl.when(z < 7)(lambda: z_up(zs, piece).start())
            spread(zs)

        @pl.when(z + distance < 8)
        def _():
            zs = z + distance
            for piece in range(2):
                arrived(block_index(y, zs, c), piece, piece)
                pl.when(z > 0)(lambda: z_down(zs, piece).start())
            spread(zs)

    def step_y(k):
        zs = place(k)
        arrived(block_index(y_prev, zs, c))
        y_on_up(zs).start()
        to_partner(y_prev, zs).start()
        arrived(block_index(y_next, zs, c))
        y_on_down(zs).start()
        to_partner(y_next, zs).start()

    def step_y_far(k):
        zs = place(k)
        arrived(block_index(y_far, zs, c), 0, 0)
        arrived(block_index(y_far, zs, c), 1, 1)
        to_partner(y_far, zs).start()

    def side(slot):
        return 2 * ((slot // 4 + slot) % 2)

    def along_x(place):
        return {"ctx": ctx, "tp": zh * 4 + place % 4}

    def far_copy(slot):
        return remote(pb.at[(x + 2) % 4, slot], xf.at[slot], xf_send.at[slot], xf_recv.at[slot],
                      along_x(x + 3 + side(slot)))

    def direct_copy(slot):
        owner = (x + 1 + side(slot)) % 4
        return remote(pb.at[owner, slot], xr.at[0, slot], xd_send.at[slot], xd_recv.at[slot], along_x(owner))

    def relay_copy(slot):
        owner = (x + 3 + side(slot)) % 4
        return remote(pb.at[owner, slot], xr.at[1, slot], xl_send.at[slot], xl_recv.at[slot], along_x(owner))

    def z_copy(i):
        return remote(zs_buf.at[i], zr_buf.at[i], zx_send.at[i], zx_recv.at[i], other_half)

    def unit(k, dy):
        zs, ys = place(k), (y + dy) % 4
        arrived(block_index(ys, zs, 1 - c))
        block = wbuf[pl.ds(pl.multiple_of((ys * 8 + zs) * 128, 128), 128), :]
        part = lax.dot_general(gated[...], block, NT, preferred_element_type=F32)
        owner, slot = (ys % 2) * 2 + zs // 4, (ys // 2) * 4 + zs % 4
        pb[owner, slot] = part.astype(BF16)
        pl.when(owner == (x + 2) % 4)(lambda: far_copy(slot).start())
        pl.when(owner == (x + 1 + side(slot)) % 4)(lambda: direct_copy(slot).start())

    def relay(k, dy):
        zs, ys = place(k), (y + dy) % 4
        owner, slot = (ys % 2) * 2 + zs // 4, (ys // 2) * 4 + zs % 4

        @pl.when(owner == (x + 3 + side(slot)) % 4)
        def _():
            far_copy(slot).wait_recv()
            pb[owner, slot] = (pb[owner, slot].astype(F32) + xf[slot].astype(F32)).astype(BF16)
            relay_copy(slot).start()

    def gather_sum(k, dy):
        zs, ys = place(k), (y + dy) % 4
        owner, slot, i = (ys % 2) * 2 + zs // 4, (ys // 2) * 4 + zs % 4, zs % 4

        @pl.when(owner == x)
        def _():
            direct_copy(slot).wait_recv()
            relay_copy(slot).wait_recv()
            total = pb[x, slot].astype(F32) + xr[0, slot].astype(F32) + xr[1, slot].astype(F32)

            @pl.when(ys // 2 == zh)
            def _():
                fin[i] = total

            @pl.when(ys // 2 != zh)
            def _():
                zs_buf[i] = total.astype(BF16)
                z_copy(i).start()

    for piece in range(2):
        pl.when(z < 7)(lambda: z_up(z, piece).start())
        pl.when(z > 0)(lambda: z_down(z, piece).start())
    spread(z)

    following = {"ctx": ctx + 1, "tp": tp}
    tail_copy = remote(qv.at[:, pl.ds(240, 16), :], halo, halo_send.at[0], halo_recv.at[0], following)
    prod_copy = remote(px.at[pl.ds(256, 128)], px.at[pl.ds(0, 128)], halo_send.at[1], halo_recv.at[1], following)
    pl.when(ctx < 63)(lambda: tail_copy.start())
    loads[2].wait()

    def lanes(ch, width=128):
        return pl.ds(pl.multiple_of(ch * width, width), width)

    def short(i, ch, first, count):
        total = None
        for j in range(7):
            term = st[i, j:j + 1, lanes(ch)] * streams[i, ch, pl.ds(16 + first - j, count), :]
            total = term if total is None else total + term
        return total

    def conv_late(ch, carry):
        for i in (1, 2):
            streams[i, ch, 16:272, :] = qv[i, :, lanes(ch)].astype(F32)
        value = short(1, ch, 128, 128) * short(2, ch, 128, 128)
        prod[128:256, lanes(ch)] = value
        px[256:384, lanes(ch)] = value.astype(BF16)
        return carry

    lax.fori_loop(0, 8, conv_late, 0)
    pl.when(ctx < 63)(lambda: prod_copy.start())

    step_z(1)

    @pl.when(ctx > 0)
    def _():
        tail_copy.wait_recv()

    @pl.when(ctx == 0)
    def _():
        halo[...] = jnp.zeros_like(halo)
        px[0:128, :] = jnp.zeros((128, 1024), BF16)

    def conv_early(ch, carry):
        for i in range(3):
            streams[i, ch, 0:16, :] = halo[i, :, lanes(ch)].astype(F32)
        streams[0, ch, 16:272, :] = qv[0, :, lanes(ch)].astype(F32)
        value = short(1, ch, 0, 128) * short(2, ch, 0, 128)
        prod[0:128, lanes(ch)] = value
        px[128:256, lanes(ch)] = value.astype(BF16)
        query[0:128, lanes(ch)] = short(0, ch, 0, 128)
        query[128:256, lanes(ch)] = short(0, ch, 128, 128)
        return carry

    lax.fori_loop(0, 8, conv_early, 0)
    step_z(2)
    step_y(0)
    step_y(1)

    for load in loads[3:]:
        load.wait()
    pl.when(ctx > 0)(lambda: prod_copy.wait_recv())

    def medium(group, carry):
        at = lanes(group, 256)
        taps = mt[:, at]
        taps_high = taps.astype(BF16)
        taps_low = (taps - taps_high.astype(F32)).astype(BF16)
        spectrum = (dot(fwd[0, :, 0:128], taps_high) + dot(fwd[0, :, 0:128], taps_low)
                    + dot(fwd[1, :, 0:128], taps_high))
        first = lax.broadcasted_iota(jnp.int32, (128, 256), 0) == 0
        h_real, h_imag = spectrum[0:128], spectrum[128:256]
        h_cross = jnp.where(first, 0.0, h_imag)
        h_last = jnp.where(first, h_imag, h_real)
        for part in range(2):
            seg = px[128 * part:128 * part + 256, at]
            x_all = dot(fwd[0], seg) + dot(fwd[1], seg)
            x_real, x_imag = x_all[0:128], x_all[128:256]
            spec[0:128, :] = x_real * h_real - x_imag * h_cross
            spec[128:256, :] = x_real * h_cross + x_imag * h_last
            whole = spec[...]
            high = whole.astype(BF16)
            low_part = (whole - high.astype(F32)).astype(BF16)
            carried = dot(inv[0], high) + dot(inv[0], low_part) + dot(inv[1], high)
            here = slice(128 * part, 128 * part + 128)
            gated[here, at] = (query[here, at] * (carried + gain[0:1, at] * prod[here, at])).astype(BF16)
        return carry

    lax.fori_loop(0, 4, medium, 0)

    def within(t, lag, run):
        pl.when((t >= lag) & (t < 8 + lag))(lambda: run(t - lag))

    def beside(run):
        def three(k):
            for dy in (0, 1, 3):
                run(k, dy)
        return three

    def across(run):
        return lambda k: run(k, 2)

    def main(t, carry):
        within(t, 0, step_z)
        within(t, 1, step_y)
        within(t, 3, step_y_far)
        within(t, 4, beside(relay))
        within(t, 6, across(relay))
        within(t, 6, beside(gather_sum))
        within(t, 8, across(gather_sum))
        within(t, 2, beside(unit))
        within(t, 4, across(unit))
        return carry

    for dy in (0, 1, 3):
        unit(0, dy)

    lax.fori_loop(3, 16, main, 0)

    for i in range(4):
        z_copy(i).wait_recv()
        out_ref[:, 128 * i:128 * i + 128] = (fin[i] + zr_buf[i].astype(F32)).astype(BF16)

    def drain(zs, carry):
        for piece in range(2):
            pl.when((zs <= z) & (z < 7))(lambda: z_up(zs, piece).wait_send())
            pl.when((zs >= z) & (z > 0))(lambda: z_down(zs, piece).wait_send())
        for copy in (y_up, y_down, y_on_up, y_on_down):
            copy(zs).wait_send()
        for ys in range(4):
            to_partner(ys, zs).wait_send()
        for copy in (far_copy, direct_copy, relay_copy):
            copy(zs).wait_send()
        return carry

    lax.fori_loop(0, 8, drain, 0)
    for i in range(4):
        z_copy(i).wait_send()

    @pl.when(ctx < 63)
    def _():
        tail_copy.wait_send()
        prod_copy.wait_send()


def on_device(qkv_values, short_taps, medium_taps, skip_gain, out_weight):
    forward, inverse = dft_tables()
    dma = pltpu.SemaphoreType.DMA
    return pl.pallas_call(
        kernel,
        out_shape=jax.ShapeDtypeStruct((256, 512), BF16),
        in_specs=[pl.BlockSpec(memory_space=pl.ANY)] * 7,
        out_specs=pl.BlockSpec(memory_space=pltpu.VMEM),
        scratch_shapes=[
            pltpu.VMEM((3, 256, 1024), BF16),
            pltpu.VMEM((3, 7, 1024), F32),
            pltpu.VMEM((128, 1024), F32),
            pltpu.VMEM((1, 1024), F32),
            pltpu.VMEM((2, 256, 256), BF16),
            pltpu.VMEM((2, 128, 256), BF16),
            pltpu.VMEM((3, 16, 1024), BF16),
            pltpu.VMEM((3, 8, 272, 128), F32),
            pltpu.VMEM((256, 1024), F32),
            pltpu.VMEM((384, 1024), BF16),
            pltpu.VMEM((256, 1024), F32),
            pltpu.VMEM((256, 256), F32),
            pltpu.VMEM((256, 1024), BF16),
            pltpu.VMEM((4096, 1024), BF16),
            pltpu.VMEM((4, 8, 256, 128), BF16),
            pltpu.VMEM((8, 256, 128), BF16),
            pltpu.VMEM((2, 8, 256, 128), BF16),
            pltpu.VMEM((4, 256, 128), F32),
            pltpu.VMEM((4, 256, 128), BF16),
            pltpu.VMEM((4, 256, 128), BF16),
            dma((7,)),
            dma((2,)), dma((2,)),
            dma((64, 2)),
            dma((2, 8, 2)), dma((2, 8)), dma((2, 8)), dma((4, 8)),
            dma((8,)), dma((8,)), dma((8,)), dma((8,)), dma((8,)), dma((8,)),
            dma((4,)), dma((4,)),
        ],
        compiler_params=pltpu.CompilerParams(
            collective_id=0, has_side_effects=True, vmem_limit_bytes=63 * 2**20),
        cost_estimate=pl.CostEstimate(flops=3 * 10**9, bytes_accessed=4 * 10**6, transcendentals=0),
    )(
        jnp.transpose(qkv_values, (1, 0, 2)),
        jnp.transpose(short_taps, (1, 0, 2)),
        medium_taps,
        skip_gain.reshape(1, -1),
        out_weight.T,
        jnp.asarray(forward),
        jnp.asarray(inverse),
    )


def solution(mesh):
    return jax.shard_map(
        on_device,
        mesh=mesh,
        in_specs=(
            P("ctx", None, "tp"),
            P(None, None, "tp"),
            P(None, "tp"),
            P("tp"),
            P("tp", "ctx"),
        ),
        out_specs=P("ctx", "tp"),
        check_vma=False,
    )
```

```python
import numpy as np
import jax
import jax.numpy as jnp
from jax import lax
from jax.experimental import pallas as pl
from jax.experimental.pallas import tpu as pltpu
from jax.sharding import PartitionSpec as P

MESH = pl.DeviceIdType.MESH
F32, BF16 = jnp.float32, jnp.bfloat16
NT = (((1,), (1,)), ((), ()))


def dft_tables():
    n = np.arange(256)
    k = np.arange(128)[:, None]
    angle = 2 * np.pi * ((k * n) % 256) / 256
    imag = -np.sin(angle)
    imag[0] = 1 - 2 * (n % 2)
    forward = np.concatenate([np.cos(angle), imag], axis=0)
    weight = np.full((256, 1), 2 / 256)
    weight[0] = weight[128] = 1 / 256
    inverse = (forward * weight).T[128:]

    def split(table):
        high = table.astype(jnp.bfloat16)
        return np.stack([high, (table - high.astype(np.float64)).astype(jnp.bfloat16)])

    return split(forward), split(inverse)


def dot(a, b):
    return jnp.dot(a, b, preferred_element_type=F32)


def kernel(q_hbm, st_hbm, mt_hbm, gain_hbm, w_hbm, f_hbm, i_hbm, out_ref,
           qv, st, mt, gain, fwd, inv, halo, streams, prod, px, query, spec, gated,
           wbuf, pb, xf, xr, fin, zs_buf, zr_buf,
           load_sem, halo_send, halo_recv, wr, s_z, s_y, s_f, s_p, xf_send, xf_recv, xd_send, xd_recv, xl_send, xl_recv, zx_send, zx_recv):
    ctx, tp = lax.axis_index("ctx"), lax.axis_index("tp")
    y, z, c = ctx // 16, (ctx // 2) % 8, ctx % 2
    zh, x = tp // 4, tp % 4

    def dev(yy, zz, cc):
        return {"ctx": (yy * 8 + zz) * 2 + cc, "tp": tp}

    y_next, y_prev, y_far = (y + 1) % 4, (y + 3) % 4, (y + 2) % 4
    other_half = {"ctx": ctx, "tp": (1 - zh) * 4 + x}

    def block_index(ys, zs, cc):
        return (ys * 8 + zs) * 2 + cc

    def rows_of(b):
        return pl.ds(pl.multiple_of(b * 64, 64), 64)

    own = block_index(y, z, c)
    loads = [
        pltpu.make_async_copy(w_hbm, wbuf.at[rows_of(own)], load_sem.at[0]),
        pltpu.make_async_copy(q_hbm, qv, load_sem.at[1]),
        pltpu.make_async_copy(st_hbm, st, load_sem.at[2]),
        pltpu.make_async_copy(mt_hbm, mt, load_sem.at[3]),
        pltpu.make_async_copy(gain_hbm, gain, load_sem.at[4]),
        pltpu.make_async_copy(f_hbm, fwd, load_sem.at[5]),
        pltpu.make_async_copy(i_hbm, inv, load_sem.at[6]),
    ]
    for load in loads:
        load.start()

    barrier = pltpu.get_barrier_semaphore()

    def greet(target):
        pl.semaphore_signal(barrier, inc=1, device_id=target, device_id_type=MESH)

    greet(other_half)
    pl.when(ctx > 0)(lambda: greet({"ctx": ctx - 1, "tp": tp}))
    pl.when(z > 0)(lambda: greet(dev(y, z - 1, c)))
    pl.when(z < 7)(lambda: greet(dev(y, z + 1, c)))
    greet(dev(y_next, z, c))
    greet(dev(y_prev, z, c))
    for step in range(1, 4):
        greet({"ctx": ctx, "tp": zh * 4 + (x + step) % 4})
    greet(dev(y, z, 1 - c))
    loads[0].wait()
    loads[1].wait()
    pl.semaphore_wait(barrier, 7 + (1 - z // 7) + (z + 7) // 8 + (1 - ctx // 63))

    def remote(src, dst, send, recv, target):
        return pltpu.make_async_remote_copy(
            src_ref=src, dst_ref=dst, send_sem=send, recv_sem=recv, device_id=target, device_id_type=MESH)

    def block_copy(b, send, target, half=0, piece=None):
        rows = rows_of(b) if piece is None else pl.ds(pl.multiple_of(b * 64 + piece * 32, 32), 32)
        return remote(wbuf.at[rows], wbuf.at[rows], send, wr.at[b, half], target)

    def z_up(zs, piece):
        return block_copy(block_index(y, zs, c), s_z.at[0, zs, piece], dev(y, z + 1, c), piece, piece)

    def z_down(zs, piece):
        return block_copy(block_index(y, zs, c), s_z.at[1, zs, piece], dev(y, z - 1, c), piece, piece)

    def y_up(zs):
        return block_copy(block_index(y, zs, c), s_y.at[0, zs], dev(y_next, z, c))

    def y_down(zs):
        return block_copy(block_index(y, zs, c), s_y.at[1, zs], dev(y_prev, z, c))

    def y_on_up(zs):
        return block_copy(block_index(y_prev, zs, c), s_f.at[0, zs], dev(y_next, z, c), 0, 0)

    def y_on_down(zs):
        return block_copy(block_index(y_next, zs, c), s_f.at[1, zs], dev(y_prev, z, c), 1, 1)

    def to_partner(ys, zs):
        return block_copy(block_index(ys, zs, c), s_p.at[ys, zs], dev(y, z, 1 - c))

    def arrived(b, half=0, piece=None):
        block_copy(b, s_p.at[0, 0], dev(y, z, 1 - c), half, piece).wait_recv()

    low = 1 - z // 4
    near = z * low + (7 - z) * (1 - low)

    def place(k):
        far = (k - 2 * near + 15) // 16
        return z + (1 - far) * ((k + 1) // 2) * (1 - 2 * ((k + 1) % 2)) + far * (k - near) * (2 * low - 1)

    def spread(zs):
        y_up(zs).start()
        y_down(zs).start()
        to_partner(y, zs).start()

    def step_z(distance):
        @pl.when(z >= distance)
        def _():
            zs = z - distance
            for piece in range(2):
                arrived(block_index(y, zs, c), piece, piece)
                pl.when(z < 7)(lambda: z_up(zs, piece).start())
            spread(zs)

        @pl.when(z + distance < 8)
        def _():
            zs = z + distance
            for piece in range(2):
                arrived(block_index(y, zs, c), piece, piece)
                pl.when(z > 0)(lambda: z_down(zs, piece).start())
            spread(zs)

    def step_y(k):
        zs = place(k)
        arrived(block_index(y_prev, zs, c))
        y_on_up(zs).start()
        to_partner(y_prev, zs).start()
        arrived(block_index(y_next, zs, c))
        y_on_down(zs).start()
        to_partner(y_next, zs).start()

    def step_y_far(k):
        zs = place(k)
        arrived(block_index(y_far, zs, c), 0, 0)
        arrived(block_index(y_far, zs, c), 1, 1)
        to_partner(y_far, zs).start()

    def side(slot):
        return 2 * ((slot // 4 + slot) % 2)

    def along_x(place):
        return {"ctx": ctx, "tp": zh * 4 + place % 4}

    def far_copy(slot):
        return remote(pb.at[(x + 2) % 4, slot], xf.at[slot], xf_send.at[slot], xf_recv.at[slot],
                      along_x(x + 3 + side(slot)))

    def direct_copy(slot):
        owner = (x + 1 + side(slot)) % 4
        return remote(pb.at[owner, slot], xr.at[0, slot], xd_send.at[slot], xd_recv.at[slot], along_x(owner))

    def relay_copy(slot):
        owner = (x + 3 + side(slot)) % 4
        return remote(pb.at[owner, slot], xr.at[1, slot], xl_send.at[slot], xl_recv.at[slot], along_x(owner))

    def z_copy(i):
        return remote(zs_buf.at[i], zr_buf.at[i], zx_send.at[i], zx_recv.at[i], other_half)

    def unit(k, dy):
        zs, ys = place(k), (y + dy) % 4
        arrived(block_index(ys, zs, 1 - c))
        block = wbuf[pl.ds(pl.multiple_of((ys * 8 + zs) * 128, 128), 128), :]
        part = lax.dot_general(gated[...], block, NT, preferred_element_type=F32)
        owner, slot = (ys % 2) * 2 + zs // 4, (ys // 2) * 4 + zs % 4
        pb[owner, slot] = part.astype(BF16)
        pl.when(owner == (x + 2) % 4)(lambda: far_copy(slot).start())
        pl.when(owner == (x + 1 + side(slot)) % 4)(lambda: direct_copy(slot).start())

    def relay(k, dy):
        zs, ys = place(k), (y + dy) % 4
        owner, slot = (ys % 2) * 2 + zs // 4, (ys // 2) * 4 + zs % 4

        @pl.when(owner == (x + 3 + side(slot)) % 4)
        def _():
            far_copy(slot).wait_recv()
            pb[owner, slot] = (pb[owner, slot].astype(F32) + xf[slot].astype(F32)).astype(BF16)
            relay_copy(slot).start()

    def gather_sum(k, dy):
        zs, ys = place(k), (y + dy) % 4
        owner, slot, i = (ys % 2) * 2 + zs // 4, (ys // 2) * 4 + zs % 4, zs % 4

        @pl.when(owner == x)
        def _():
            direct_copy(slot).wait_recv()
            relay_copy(slot).wait_recv()
            total = pb[x, slot].astype(F32) + xr[0, slot].astype(F32) + xr[1, slot].astype(F32)

            @pl.when(ys // 2 == zh)
            def _():
                fin[i] = total

            @pl.when(ys // 2 != zh)
            def _():
                zs_buf[i] = total.astype(BF16)
                z_copy(i).start()

    for piece in range(2):
        pl.when(z < 7)(lambda: z_up(z, piece).start())
        pl.when(z > 0)(lambda: z_down(z, piece).start())
    spread(z)

    following = {"ctx": ctx + 1, "tp": tp}
    tail_copy = remote(qv.at[:, pl.ds(240, 16), :], halo, halo_send.at[0], halo_recv.at[0], following)
    prod_copy = remote(px.at[pl.ds(256, 128)], px.at[pl.ds(0, 128)], halo_send.at[1], halo_recv.at[1], following)
    pl.when(ctx < 63)(lambda: tail_copy.start())
    loads[2].wait()

    def lanes(ch, width=128):
        return pl.ds(pl.multiple_of(ch * width, width), width)

    def short(i, ch, first, count):
        total = None
        for j in range(7):
            term = st[i, j:j + 1, lanes(ch)] * streams[i, ch, pl.ds(16 + first - j, count), :]
            total = term if total is None else total + term
        return total

    def conv_late(ch, carry):
        for i in (1, 2):
            streams[i, ch, 16:272, :] = qv[i, :, lanes(ch)].astype(F32)
        value = short(1, ch, 128, 128) * short(2, ch, 128, 128)
        prod[128:256, lanes(ch)] = value
        px[256:384, lanes(ch)] = value.astype(BF16)
        return carry

    lax.fori_loop(0, 8, conv_late, 0)
    pl.when(ctx < 63)(lambda: prod_copy.start())

    step_z(1)

    @pl.when(ctx > 0)
    def _():
        tail_copy.wait_recv()

    @pl.when(ctx == 0)
    def _():
        halo[...] = jnp.zeros_like(halo)
        px[0:128, :] = jnp.zeros((128, 1024), BF16)

    def conv_early(ch, carry):
        for i in range(3):
            streams[i, ch, 0:16, :] = halo[i, :, lanes(ch)].astype(F32)
        streams[0, ch, 16:272, :] = qv[0, :, lanes(ch)].astype(F32)
        value = short(1, ch, 0, 128) * short(2, ch, 0, 128)
        prod[0:128, lanes(ch)] = value
        px[128:256, lanes(ch)] = value.astype(BF16)
        query[0:128, lanes(ch)] = short(0, ch, 0, 128)
        query[128:256, lanes(ch)] = short(0, ch, 128, 128)
        return carry

    lax.fori_loop(0, 8, conv_early, 0)
    step_z(2)
    step_y(0)
    step_y(1)

    for load in loads[3:]:
        load.wait()
    pl.when(ctx > 0)(lambda: prod_copy.wait_recv())

    def medium(group, carry):
        at = lanes(group, 256)
        taps = mt[:, at]
        taps_high = taps.astype(BF16)
        taps_low = (taps - taps_high.astype(F32)).astype(BF16)
        spectrum = (dot(fwd[0, :, 0:128], taps_high) + dot(fwd[0, :, 0:128], taps_low)
                    + dot(fwd[1, :, 0:128], taps_high))
        first = lax.broadcasted_iota(jnp.int32, (128, 256), 0) == 0
        h_real, h_imag = spectrum[0:128], spectrum[128:256]
        h_cross = jnp.where(first, 0.0, h_imag)
        h_last = jnp.where(first, h_imag, h_real)
        for part in range(2):
            seg = px[128 * part:128 * part + 256, at]
            x_all = dot(fwd[0], seg) + dot(fwd[1], seg)
            x_real, x_imag = x_all[0:128], x_all[128:256]
            spec[0:128, :] = x_real * h_real - x_imag * h_cross
            spec[128:256, :] = x_real * h_cross + x_imag * h_last
            whole = spec[...]
            high = whole.astype(BF16)
            low_part = (whole - high.astype(F32)).astype(BF16)
            carried = dot(inv[0], high) + dot(inv[0], low_part) + dot(inv[1], high)
            here = slice(128 * part, 128 * part + 128)
            gated[here, at] = (query[here, at] * (carried + gain[0:1, at] * prod[here, at])).astype(BF16)
        return carry

    lax.fori_loop(0, 4, medium, 0)

    def within(t, lag, run):
        pl.when((t >= lag) & (t < 8 + lag))(lambda: run(t - lag))

    def beside(run):
        def three(k):
            for dy in (0, 1, 3):
                run(k, dy)
        return three

    def across(run):
        return lambda k: run(k, 2)

    def main(t, carry):
        within(t, 0, step_z)
        within(t, 1, step_y)
        within(t, 3, step_y_far)
        within(t, 8, across(gather_sum))
        within(t, 6, beside(gather_sum))
        within(t, 6, across(relay))
        within(t, 4, beside(relay))
        within(t, 4, across(unit))
        within(t, 2, beside(unit))
        return carry

    for dy in (0, 1, 3):
        unit(0, dy)

    lax.fori_loop(3, 16, main, 0)

    for i in range(4):
        z_copy(i).wait_recv()
        out_ref[:, 128 * i:128 * i + 128] = (fin[i] + zr_buf[i].astype(F32)).astype(BF16)

    def drain(zs, carry):
        for piece in range(2):
            pl.when((zs <= z) & (z < 7))(lambda: z_up(zs, piece).wait_send())
            pl.when((zs >= z) & (z > 0))(lambda: z_down(zs, piece).wait_send())
        for copy in (y_up, y_down, y_on_up, y_on_down):
            copy(zs).wait_send()
        for ys in range(4):
            to_partner(ys, zs).wait_send()
        for copy in (far_copy, direct_copy, relay_copy):
            copy(zs).wait_send()
        return carry

    lax.fori_loop(0, 8, drain, 0)
    for i in range(4):
        z_copy(i).wait_send()

    @pl.when(ctx < 63)
    def _():
        tail_copy.wait_send()
        prod_copy.wait_send()


def on_device(qkv_values, short_taps, medium_taps, skip_gain, out_weight):
    forward, inverse = dft_tables()
    dma = pltpu.SemaphoreType.DMA
    return pl.pallas_call(
        kernel,
        out_shape=jax.ShapeDtypeStruct((256, 512), BF16),
        in_specs=[pl.BlockSpec(memory_space=pl.ANY)] * 7,
        out_specs=pl.BlockSpec(memory_space=pltpu.VMEM),
        scratch_shapes=[
            pltpu.VMEM((3, 256, 1024), BF16),
            pltpu.VMEM((3, 7, 1024), F32),
            pltpu.VMEM((128, 1024), F32),
            pltpu.VMEM((1, 1024), F32),
            pltpu.VMEM((2, 256, 256), BF16),
            pltpu.VMEM((2, 128, 256), BF16),
            pltpu.VMEM((3, 16, 1024), BF16),
            pltpu.VMEM((3, 8, 272, 128), F32),
            pltpu.VMEM((256, 1024), F32),
            pltpu.VMEM((384, 1024), BF16),
            pltpu.VMEM((256, 1024), F32),
            pltpu.VMEM((256, 256), F32),
            pltpu.VMEM((256, 1024), BF16),
            pltpu.VMEM((4096, 1024), BF16),
            pltpu.VMEM((4, 8, 256, 128), BF16),
            pltpu.VMEM((8, 256, 128), BF16),
            pltpu.VMEM((2, 8, 256, 128), BF16),
            pltpu.VMEM((4, 256, 128), F32),
            pltpu.VMEM((4, 256, 128), BF16),
            pltpu.VMEM((4, 256, 128), BF16),
            dma((7,)),
            dma((2,)), dma((2,)),
            dma((64, 2)),
            dma((2, 8, 2)), dma((2, 8)), dma((2, 8)), dma((4, 8)),
            dma((8,)), dma((8,)), dma((8,)), dma((8,)), dma((8,)), dma((8,)),
            dma((4,)), dma((4,)),
        ],
        compiler_params=pltpu.CompilerParams(
            collective_id=0, has_side_effects=True, vmem_limit_bytes=63 * 2**20),
        cost_estimate=pl.CostEstimate(flops=3 * 10**9, bytes_accessed=4 * 10**6, transcendentals=0),
    )(
        jnp.transpose(qkv_values, (1, 0, 2)),
        jnp.transpose(short_taps, (1, 0, 2)),
        medium_taps,
        skip_gain.reshape(1, -1),
        out_weight.T,
        jnp.asarray(forward),
        jnp.asarray(inverse),
    )


def solution(mesh):
    return jax.shard_map(
        on_device,
        mesh=mesh,
        in_specs=(
            P("ctx", None, "tp"),
            P(None, None, "tp"),
            P(None, "tp"),
            P("tp"),
            P("tp", "ctx"),
        ),
        out_specs=P("ctx", "tp"),
        check_vma=False,
    )
```

```python
import numpy as np
import jax
import jax.numpy as jnp
from jax import lax
from jax.experimental import pallas as pl
from jax.experimental.pallas import tpu as pltpu
from jax.sharding import PartitionSpec as P

MESH = pl.DeviceIdType.MESH
F32, BF16 = jnp.float32, jnp.bfloat16
NT = (((1,), (1,)), ((), ()))


def dft_tables():
    n = np.arange(256)
    k = np.arange(128)[:, None]
    angle = 2 * np.pi * ((k * n) % 256) / 256
    imag = -np.sin(angle)
    imag[0] = 1 - 2 * (n % 2)
    forward = np.concatenate([np.cos(angle), imag], axis=0)
    weight = np.full((256, 1), 2 / 256)
    weight[0] = weight[128] = 1 / 256
    inverse = (forward * weight).T[128:]

    def split(table):
        high = table.astype(jnp.bfloat16)
        return np.stack([high, (table - high.astype(np.float64)).astype(jnp.bfloat16)])

    return split(forward), split(inverse)


def dot(a, b):
    return jnp.dot(a, b, preferred_element_type=F32)


def kernel(q_hbm, st_hbm, mt_hbm, gain_hbm, w_hbm, f_hbm, i_hbm, out_ref,
           qv, st, mt, gain, fwd, inv, halo, streams, prod, px, query, spec, gated,
           wbuf, pb, xf, xr, fin, zs_buf, zr_buf,
           load_sem, halo_send, halo_recv, wr, s_z, s_y, s_f, s_p, xf_send, xf_recv, xd_send, xd_recv, xl_send, xl_recv, zx_send, zx_recv):
    ctx, tp = lax.axis_index("ctx"), lax.axis_index("tp")
    y, z, c = ctx // 16, (ctx // 2) % 8, ctx % 2
    zh, x = tp // 4, tp % 4

    def dev(yy, zz, cc):
        return {"ctx": (yy * 8 + zz) * 2 + cc, "tp": tp}

    y_next, y_prev, y_far = (y + 1) % 4, (y + 3) % 4, (y + 2) % 4
    other_half = {"ctx": ctx, "tp": (1 - zh) * 4 + x}

    def block_index(ys, zs, cc):
        return (ys * 8 + zs) * 2 + cc

    def rows_of(b):
        return pl.ds(pl.multiple_of(b * 64, 64), 64)

    own = block_index(y, z, c)
    loads = [
        pltpu.make_async_copy(w_hbm, wbuf.at[rows_of(own)], load_sem.at[0]),
        pltpu.make_async_copy(q_hbm, qv, load_sem.at[1]),
        pltpu.make_async_copy(st_hbm, st, load_sem.at[2]),
        pltpu.make_async_copy(mt_hbm, mt, load_sem.at[3]),
        pltpu.make_async_copy(gain_hbm, gain, load_sem.at[4]),
        pltpu.make_async_copy(f_hbm, fwd, load_sem.at[5]),
        pltpu.make_async_copy(i_hbm, inv, load_sem.at[6]),
    ]
    for load in loads:
        load.start()

    barrier = pltpu.get_barrier_semaphore()

    def greet(target):
        pl.semaphore_signal(barrier, inc=1, device_id=target, device_id_type=MESH)

    greet(other_half)
    pl.when(ctx > 0)(lambda: greet({"ctx": ctx - 1, "tp": tp}))
    pl.when(z > 0)(lambda: greet(dev(y, z - 1, c)))
    pl.when(z < 7)(lambda: greet(dev(y, z + 1, c)))
    greet(dev(y_next, z, c))
    greet(dev(y_prev, z, c))
    for step in range(1, 4):
        greet({"ctx": ctx, "tp": zh * 4 + (x + step) % 4})
    greet(dev(y, z, 1 - c))
    loads[0].wait()
    loads[1].wait()
    pl.semaphore_wait(barrier, 7 + (1 - z // 7) + (z + 7) // 8 + (1 - ctx // 63))

    def remote(src, dst, send, recv, target):
        return pltpu.make_async_remote_copy(
            src_ref=src, dst_ref=dst, send_sem=send, recv_sem=recv, device_id=target, device_id_type=MESH)

    def block_copy(b, send, target, half=0, piece=None):
        rows = rows_of(b) if piece is None else pl.ds(pl.multiple_of(b * 64 + piece * 32, 32), 32)
        return remote(wbuf.at[rows], wbuf.at[rows], send, wr.at[b, half], target)

    def z_up(zs, piece):
        return block_copy(block_index(y, zs, c), s_z.at[0, zs, piece], dev(y, z + 1, c), piece, piece)

    def z_down(zs, piece):
        return block_copy(block_index(y, zs, c), s_z.at[1, zs, piece], dev(y, z - 1, c), piece, piece)

    def y_up(zs):
        return block_copy(block_index(y, zs, c), s_y.at[0, zs], dev(y_next, z, c))

    def y_down(zs):
        return block_copy(block_index(y, zs, c), s_y.at[1, zs], dev(y_prev, z, c))

    def y_on_up(zs):
        return block_copy(block_index(y_prev, zs, c), s_f.at[0, zs], dev(y_next, z, c), 0, 0)

    def y_on_down(zs):
        return block_copy(block_index(y_next, zs, c), s_f.at[1, zs], dev(y_prev, z, c), 1, 1)

    def to_partner(ys, zs):
        return block_copy(block_index(ys, zs, c), s_p.at[ys, zs], dev(y, z, 1 - c))

    def arrived(b, half=0, piece=None):
        block_copy(b, s_p.at[0, 0], dev(y, z, 1 - c), half, piece).wait_recv()

    low = 1 - z // 4
    near = z * low + (7 - z) * (1 - low)

    def place(k):
        far = (k - 2 * near + 15) // 16
        return z + (1 - far) * ((k + 1) // 2) * (1 - 2 * ((k + 1) % 2)) + far * (k - near) * (2 * low - 1)

    def spread(zs):
        y_up(zs).start()
        y_down(zs).start()
        to_partner(y, zs).start()

    def step_z(distance):
        @pl.when(z >= distance)
        def _():
            zs = z - distance
            for piece in range(2):
                arrived(block_index(y, zs, c), piece, piece)
                pl.when(z < 7)(lambda: z_up(zs, piece).start())
            spread(zs)

        @pl.when(z + distance < 8)
        def _():
            zs = z + distance
            for piece in range(2):
                arrived(block_index(y, zs, c), piece, piece)
                pl.when(z > 0)(lambda: z_down(zs, piece).start())
            spread(zs)

    def step_y(k):
        zs = place(k)
        arrived(block_index(y_prev, zs, c))
        y_on_up(zs).start()
        to_partner(y_prev, zs).start()
        arrived(block_index(y_next, zs, c))
        y_on_down(zs).start()
        to_partner(y_next, zs).start()

    def step_y_far(k):
        zs = place(k)
        arrived(block_index(y_far, zs, c), 0, 0)
        arrived(block_index(y_far, zs, c), 1, 1)
        to_partner(y_far, zs).start()

    def side(slot):
        return 2 * ((slot // 4 + slot) % 2)

    def along_x(place):
        return {"ctx": ctx, "tp": zh * 4 + place % 4}

    def far_copy(slot):
        return remote(pb.at[(x + 2) % 4, slot], xf.at[slot], xf_send.at[slot], xf_recv.at[slot],
                      along_x(x + 3 + side(slot)))

    def direct_copy(slot):
        owner = (x + 1 + side(slot)) % 4
        return remote(pb.at[owner, slot], xr.at[0, slot], xd_send.at[slot], xd_recv.at[slot], along_x(owner))

    def relay_copy(slot):
        owner = (x + 3 + side(slot)) % 4
        return remote(pb.at[owner, slot], xr.at[1, slot], xl_send.at[slot], xl_recv.at[slot], along_x(owner))

    def z_copy(i):
        return remote(zs_buf.at[i], zr_buf.at[i], zx_send.at[i], zx_recv.at[i], other_half)

    def unit(k, dy):
        zs, ys = place(k), (y + dy) % 4
        arrived(block_index(ys, zs, 1 - c))
        block = wbuf[pl.ds(pl.multiple_of((ys * 8 + zs) * 128, 128), 128), :]
        part = lax.dot_general(gated[...], block, NT, preferred_element_type=F32)
        owner, slot = (ys % 2) * 2 + zs // 4, (ys // 2) * 4 + zs % 4
        pb[owner, slot] = part.astype(BF16)
        pl.when(owner == (x + 2) % 4)(lambda: far_copy(slot).start())
        pl.when(owner == (x + 1 + side(slot)) % 4)(lambda: direct_copy(slot).start())

    def relay(k, dy):
        zs, ys = place(k), (y + dy) % 4
        owner, slot = (ys % 2) * 2 + zs // 4, (ys // 2) * 4 + zs % 4

        @pl.when(owner == (x + 3 + side(slot)) % 4)
        def _():
            far_copy(slot).wait_recv()
            pb[owner, slot] = (pb[owner, slot].astype(F32) + xf[slot].astype(F32)).astype(BF16)
            relay_copy(slot).start()

    def gather_sum(k, dy):
        zs, ys = place(k), (y + dy) % 4
        owner, slot, i = (ys % 2) * 2 + zs // 4, (ys // 2) * 4 + zs % 4, zs % 4

        @pl.when(owner == x)
        def _():
            direct_copy(slot).wait_recv()
            relay_copy(slot).wait_recv()
            total = pb[x, slot].astype(F32) + xr[0, slot].astype(F32) + xr[1, slot].astype(F32)

            @pl.when(ys // 2 == zh)
            def _():
                fin[i] = total

            @pl.when(ys // 2 != zh)
            def _():
                zs_buf[i] = total.astype(BF16)
                z_copy(i).start()

    for piece in range(2):
        pl.when(z < 7)(lambda: z_up(z, piece).start())
        pl.when(z > 0)(lambda: z_down(z, piece).start())
    spread(z)

    following = {"ctx": ctx + 1, "tp": tp}
    tail_copy = remote(qv.at[:, pl.ds(240, 16), :], halo, halo_send.at[0], halo_recv.at[0], following)
    prod_copy = remote(px.at[pl.ds(256, 128)], px.at[pl.ds(0, 128)], halo_send.at[1], halo_recv.at[1], following)
    pl.when(ctx < 63)(lambda: tail_copy.start())
    loads[2].wait()

    def lanes(ch, width=128):
        return pl.ds(pl.multiple_of(ch * width, width), width)

    def short(i, ch, first, count):
        total = None
        for j in range(7):
            term = st[i, j:j + 1, lanes(ch)] * streams[i, ch, pl.ds(16 + first - j, count), :]
            total = term if total is None else total + term
        return total

    def conv_late(ch, carry):
        for i in (1, 2):
            streams[i, ch, 16:272, :] = qv[i, :, lanes(ch)].astype(F32)
        value = short(1, ch, 128, 128) * short(2, ch, 128, 128)
        prod[128:256, lanes(ch)] = value
        px[256:384, lanes(ch)] = value.astype(BF16)
        return carry

    lax.fori_loop(0, 8, conv_late, 0)
    pl.when(ctx < 63)(lambda: prod_copy.start())

    step_z(1)

    @pl.when(ctx > 0)
    def _():
        tail_copy.wait_recv()

    @pl.when(ctx == 0)
    def _():
        halo[...] = jnp.zeros_like(halo)
        px[0:128, :] = jnp.zeros((128, 1024), BF16)

    def conv_early(ch, carry):
        for i in range(3):
            streams[i, ch, 0:16, :] = halo[i, :, lanes(ch)].astype(F32)
        streams[0, ch, 16:272, :] = qv[0, :, lanes(ch)].astype(F32)
        value = short(1, ch, 0, 128) * short(2, ch, 0, 128)
        prod[0:128, lanes(ch)] = value
        px[128:256, lanes(ch)] = value.astype(BF16)
        query[0:128, lanes(ch)] = short(0, ch, 0, 128)
        query[128:256, lanes(ch)] = short(0, ch, 128, 128)
        return carry

    lax.fori_loop(0, 8, conv_early, 0)
    step_z(2)
    step_y(0)
    step_y(1)

    for load in loads[3:]:
        load.wait()
    pl.when(ctx > 0)(lambda: prod_copy.wait_recv())

    def medium(group, carry):
        at = lanes(group, 256)
        taps = mt[:, at]
        taps_high = taps.astype(BF16)
        taps_low = (taps - taps_high.astype(F32)).astype(BF16)
        spectrum = (dot(fwd[0, :, 0:128], taps_high) + dot(fwd[0, :, 0:128], taps_low)
                    + dot(fwd[1, :, 0:128], taps_high))
        first = lax.broadcasted_iota(jnp.int32, (128, 256), 0) == 0
        h_real, h_imag = spectrum[0:128], spectrum[128:256]
        h_cross = jnp.where(first, 0.0, h_imag)
        h_last = jnp.where(first, h_imag, h_real)
        for part in range(2):
            seg = px[128 * part:128 * part + 256, at]
            x_all = dot(fwd[0], seg) + dot(fwd[1], seg)
            x_real, x_imag = x_all[0:128], x_all[128:256]
            spec[0:128, :] = x_real * h_real - x_imag * h_cross
            spec[128:256, :] = x_real * h_cross + x_imag * h_last
            whole = spec[...]
            high = whole.astype(BF16)
            low_part = (whole - high.astype(F32)).astype(BF16)
            carried = dot(inv[0], high) + dot(inv[0], low_part) + dot(inv[1], high)
            here = slice(128 * part, 128 * part + 128)
            gated[here, at] = (query[here, at] * (carried + gain[0:1, at] * prod[here, at])).astype(BF16)
        return carry

    lax.fori_loop(0, 4, medium, 0)

    def within(t, lag, run):
        pl.when((t >= lag) & (t < 8 + lag))(lambda: run(t - lag))

    def beside(run):
        def three(k):
            for dy in (0, 1, 3):
                run(k, dy)
        return three

    def across(run):
        return lambda k: run(k, 2)

    def main(t, carry):
        within(t, 0, step_z)
        within(t, 3, step_y_far)
        within(t, 1, step_y)
        within(t, 8, across(gather_sum))
        within(t, 6, beside(gather_sum))
        within(t, 6, across(relay))
        within(t, 4, beside(relay))
        within(t, 4, across(unit))
        within(t, 2, beside(unit))
        return carry

    for dy in (0, 1, 3):
        unit(0, dy)

    lax.fori_loop(3, 16, main, 0)

    for i in range(4):
        z_copy(i).wait_recv()
        out_ref[:, 128 * i:128 * i + 128] = (fin[i] + zr_buf[i].astype(F32)).astype(BF16)

    def drain(zs, carry):
        for piece in range(2):
            pl.when((zs <= z) & (z < 7))(lambda: z_up(zs, piece).wait_send())
            pl.when((zs >= z) & (z > 0))(lambda: z_down(zs, piece).wait_send())
        for copy in (y_up, y_down, y_on_up, y_on_down):
            copy(zs).wait_send()
        for ys in range(4):
            to_partner(ys, zs).wait_send()
        for copy in (far_copy, direct_copy, relay_copy):
            copy(zs).wait_send()
        return carry

    lax.fori_loop(0, 8, drain, 0)
    for i in range(4):
        z_copy(i).wait_send()

    @pl.when(ctx < 63)
    def _():
        tail_copy.wait_send()
        prod_copy.wait_send()


def on_device(qkv_values, short_taps, medium_taps, skip_gain, out_weight):
    forward, inverse = dft_tables()
    dma = pltpu.SemaphoreType.DMA
    return pl.pallas_call(
        kernel,
        out_shape=jax.ShapeDtypeStruct((256, 512), BF16),
        in_specs=[pl.BlockSpec(memory_space=pl.ANY)] * 7,
        out_specs=pl.BlockSpec(memory_space=pltpu.VMEM),
        scratch_shapes=[
            pltpu.VMEM((3, 256, 1024), BF16),
            pltpu.VMEM((3, 7, 1024), F32),
            pltpu.VMEM((128, 1024), F32),
            pltpu.VMEM((1, 1024), F32),
            pltpu.VMEM((2, 256, 256), BF16),
            pltpu.VMEM((2, 128, 256), BF16),
            pltpu.VMEM((3, 16, 1024), BF16),
            pltpu.VMEM((3, 8, 272, 128), F32),
            pltpu.VMEM((256, 1024), F32),
            pltpu.VMEM((384, 1024), BF16),
            pltpu.VMEM((256, 1024), F32),
            pltpu.VMEM((256, 256), F32),
            pltpu.VMEM((256, 1024), BF16),
            pltpu.VMEM((4096, 1024), BF16),
            pltpu.VMEM((4, 8, 256, 128), BF16),
            pltpu.VMEM((8, 256, 128), BF16),
            pltpu.VMEM((2, 8, 256, 128), BF16),
            pltpu.VMEM((4, 256, 128), F32),
            pltpu.VMEM((4, 256, 128), BF16),
            pltpu.VMEM((4, 256, 128), BF16),
            dma((7,)),
            dma((2,)), dma((2,)),
            dma((64, 2)),
            dma((2, 8, 2)), dma((2, 8)), dma((2, 8)), dma((4, 8)),
            dma((8,)), dma((8,)), dma((8,)), dma((8,)), dma((8,)), dma((8,)),
            dma((4,)), dma((4,)),
        ],
        compiler_params=pltpu.CompilerParams(
            collective_id=0, has_side_effects=True, vmem_limit_bytes=63 * 2**20),
        cost_estimate=pl.CostEstimate(flops=3 * 10**9, bytes_accessed=4 * 10**6, transcendentals=0),
    )(
        jnp.transpose(qkv_values, (1, 0, 2)),
        jnp.transpose(short_taps, (1, 0, 2)),
        medium_taps,
        skip_gain.reshape(1, -1),
        out_weight.T,
        jnp.asarray(forward),
        jnp.asarray(inverse),
    )


def solution(mesh):
    return jax.shard_map(
        on_device,
        mesh=mesh,
        in_specs=(
            P("ctx", None, "tp"),
            P(None, None, "tp"),
            P(None, "tp"),
            P("tp"),
            P("tp", "ctx"),
        ),
        out_specs=P("ctx", "tp"),
        check_vma=False,
    )
```
